32 devices in a mesh: cfg: 2 (over x), seq: 8 (over z, core), wgt: 2 (over y).
Axes of the slice: x: 2, y: 2, z: 4, core: 2. Of those that a mesh axis runs over, the one named last changes fastest.
Arguments:
- latent: float32 [1024, 4, 64], P(('seq', 'wgt'), 'cfg'), may hold values from -6 to 6
- img_hidden: bfloat16 [2, 1024, 4, 2432], P('cfg', 'seq'), may hold values from -5 to 5
- txt_hidden: bfloat16 [2, 512, 2432], P('cfg', 'seq'), may hold values from -6 to 6
- segments: int32 [2, 512], P('cfg', 'seq'), may hold values from 0 to 3, never falling along the last dimension, each value on 1 to 154 neighbouring positions
- timesteps: int32 [4], replicated, may hold values from 0 to 27
- modulation: float32 [2, 4, 10, 2432], P('cfg'), may hold values from -3 to 3
- qk_gain: float32 [2, 64], replicated, may hold values from 1.5 to 8
- qkv_weight: bfloat16 [3, 2432, 1536], P(None, 'seq', 'wgt'), may hold values from -0.08111071 to 0.08111071, as said below
- text_weight: bfloat16 [2, 2432, 1536], P(None, 'seq', 'wgt'), may hold values from -0.125 to 0.125
- out_weight: bfloat16 [1536, 2432], P('wgt', 'seq'), may hold values from -0.15625 to 0.15625
- expand_weight: bfloat16 [2432, 5632], P('seq', 'wgt'), may hold values from -0.125 to 0.125
- contract_weight: bfloat16 [5632, 2432], P('wgt', 'seq'), may hold values from -0.078125 to 0.078125
- final_weight: bfloat16 [2432, 64], replicated, may hold values from -0.0625 to 0.0625
Outputs:
- velocity: float32 [1024, 4, 64], P(('seq', 'wgt'), 'cfg')
- next_latent: float32 [1024, 4, 64], P(('seq', 'wgt'), 'cfg')
The draws below stay inside these ranges and needn't reach their ends.
Inputs may be any that keep to these rules, and one draw needn't show every extreme that they name: `segments`: along each row the segment never falls, and each request has 1 to 154 positions. `qkv_weight`: entries are of order 2432 ** -0.5.
All inputs are finite; a program needn't handle non-finite values.
Results may differ from the reference program's by a relative error of at most 0.012.
The reference program's roundings to bfloat16 on the way (of `image_normed`, `text_normed`, `attended`, `branch_in`, `expanded` and `final_in`) count: a program that leaves them out, or rounds other values in their place, can miss the bound.
Values may be sent and summed in bfloat16 or wider, within the bound.
A program may use at most 128 MiB of HBM per device.

```python
import math
import jax
import jax.numpy as jnp
import numpy as np
from jax import lax

D = 2432
HEAD = 64
CH = 64
H = 24
FF = 5632
IMG = 1024
TXT_MOST = 154
STEPS = 28
R = 4
HD = 1536
TXT_ALL = 512
N_WGT = 2


def draw_img_hidden(key, part):
    values = jax.random.truncated_normal(key, -5.0, 5.0, (2, IMG, R, D), jnp.float32)
    return values.astype(jnp.bfloat16)


def draw_qk_gain(key, part):
    return jax.random.uniform(key, (2, HEAD), jnp.float32, 1.5, 2.5)


def draw_qkv_weight(key, part):
    values = jax.random.truncated_normal(key, -4.0, 4.0, (3, D, HD), jnp.float32) * D ** (-0.5)
    return values.astype(jnp.bfloat16)


def plant(array, rng, low, top_value):
    longest = array.shape.index(max(array.shape))
    spots = []
    for shift in (0, 1):
        where = [jax.random.randint(jax.random.fold_in(rng, axis), (), 0, length) for axis, length in enumerate(array.shape)]
        where[longest] = (where[longest] + shift) % array.shape[longest]
        spots.append(tuple(where))
    return array.at[spots[0]].set(low).at[spots[1]].set(top_value)


def block_levels(key, shape, pieces, least, top_value):
    def one(axis_at, blocks):
        draws = jax.random.uniform(jax.random.fold_in(jax.random.fold_in(key, 6), axis_at), (blocks,), jnp.float32, least / len(pieces), top_value / len(pieces))
        return jnp.repeat(jnp.exp(draws), shape[axis_at] // blocks).reshape((-1,) + (1,) * (len(shape) - axis_at - 1))

    loudness = one(*pieces[0])
    for cut in pieces[1:]:
        loudness = loudness * one(*cut)
    return loudness


def split_up(amount, total, limit, slope):
    loads = [(1 << 20) // math.isqrt(rank ** slope) + 1 for rank in range(2, amount + 1)]
    spare, counts = total - limit - (amount - 1), [1] * (amount - 1)
    while spare > 0:
        candidates = [i for i in range(amount - 1) if counts[i] < limit]
        whole, left = sum([loads[i] for i in candidates]), spare
        for i in candidates:
            addition = min(limit - counts[i], max(1, left * loads[i] // whole), spare)
            counts[i] = counts[i] + addition
            spare = spare - addition
    return np.array([limit] + counts)


def ragged(key, count, total, reach, skew):
    if count == 2:
        one = jax.random.randint(key, (), max(1, total - reach), min(reach, total - 1) + 1)
        return jnp.stack([one, total - one])
    lengths = jnp.asarray(split_up(count, total, reach, skew), jnp.int32)
    couples = (count - 1) // 2
    giver, taker = lengths[1:1 + 2 * couples:2], lengths[2:2 + 2 * couples:2]
    margin = jnp.minimum(giver - 1, reach - taker)
    passed = jax.random.randint(jax.random.fold_in(key, 1), (couples,), 0, 1 << 20) % (margin + 1)
    lengths = lengths.at[1:1 + 2 * couples:2].set(giver - passed).at[2:2 + 2 * couples:2].set(taker + passed)
    return lengths[jax.random.permutation(jax.random.fold_in(key, 2), count)]


def noise(own_key, extent, scale, reach, cuts=(), kind=jnp.bfloat16):
    factor_of = block_levels(own_key, extent, cuts, -0.22, 0.18) if cuts else 1.0
    values = jax.random.normal(own_key, extent, jnp.float32) * scale * factor_of
    return jnp.minimum(jnp.maximum(values, -reach), reach).astype(kind)


def setup_inputs(seed: int = 0) -> dict:
    key_of = jax.random.split(jax.random.key(seed), 14)
    latent = noise(key_of[0], (IMG, R, CH), 1.0, 6.0, ((0, 16), (1, 2)), jnp.float32)
    img_hidden = draw_img_hidden(jax.random.fold_in(key_of[13], 71), 0)
    txt_hidden = noise(key_of[2], (2, TXT_ALL, D), 1.0, 6.0, ((0, 2), (1, 8)))
    segments = jax.vmap(lambda own: jnp.searchsorted(jnp.cumsum(ragged(own, R, TXT_ALL, TXT_MOST, 1)), jnp.arange(TXT_ALL), side="right"))(jax.random.split(key_of[3], 2)).reshape((2, TXT_ALL)).astype(jnp.int32)
    timesteps = plant(jax.random.randint(key_of[4], (R,), 0, STEPS), jax.random.fold_in(key_of[4], 1), 0, STEPS - 1).astype(jnp.int32)
    modulation = noise(key_of[5], (2, R, 10, D), 0.5, 3.0, ((0, 2),), jnp.float32)
    qk_gain = draw_qk_gain(jax.random.fold_in(key_of[13], 71), 0)
    qkv_weight = draw_qkv_weight(jax.random.fold_in(key_of[13], 71), 0)
    text_weight = noise(key_of[8], (2, D, HD), D ** -0.5, 0.125, ((1, 8), (2, 2)))
    out_weight = noise(key_of[9], (HD, D), HD ** -0.5, 0.15625, ((0, 2), (1, 8)))
    expand_weight = noise(key_of[10], (D, FF), D ** -0.5, 0.125, ((0, 8), (1, 2)))
    contract_weight = noise(key_of[11], (FF, D), FF ** -0.5, 0.078125, ((0, 2), (1, 8)))
    final_weight = noise(key_of[12], (D, CH), (4 * D) ** -0.5, 0.0625)
    return {"latent": latent, "img_hidden": img_hidden, "txt_hidden": txt_hidden, "segments": segments, "timesteps": timesteps, "modulation": modulation, "qk_gain": qk_gain, "qkv_weight": qkv_weight, "text_weight": text_weight, "out_weight": out_weight, "expand_weight": expand_weight, "contract_weight": contract_weight, "final_weight": final_weight}


guidance_scale = 3.5
flow_shift = 3.0
eps_norm = 1e-06
masked_score = -1e+30

def layer_norm(values):
    center = lax.optimization_barrier(jnp.mean(values, axis=-1, keepdims=True))
    centred = values - center
    spread = lax.optimization_barrier(jnp.mean(centred * centred, axis=-1, keepdims=True))
    return centred * lax.rsqrt(spread + eps_norm)

def head_norm(values, gain_row):
    power = lax.optimization_barrier(jnp.mean(values * values, axis=-1, keepdims=True))
    return values * lax.rsqrt(power + eps_norm) * gain_row

def sigma_of(index_row):
    time_left = 1.0 - index_row.astype(jnp.float32) / STEPS
    return flow_shift * time_left / (1.0 + (flow_shift - 1.0) * time_left)

def rounded(values):
    return lax.optimization_barrier(values.astype(jnp.bfloat16)).astype(jnp.float32)

def half_velocity(hidden, text_rows, segment_row, modulate, qk_gain, qkv_weight, text_weight, out_weight, expand_weight, contract_weight, final_weight):
    hidden_f = hidden.astype(jnp.float32)
    image_normed = (layer_norm(hidden_f) * (1.0 + modulate[:, 1]) + modulate[:, 0]).astype(jnp.bfloat16)
    one_hot = (segment_row[:, None] == jnp.arange(R, dtype=jnp.int32)[None, :]).astype(jnp.float32)
    text_mod = jnp.einsum('tr,rkd->tkd', one_hot, modulate[:, 3:5], precision=lax.Precision.HIGHEST)
    text_normed = (layer_norm(text_rows.astype(jnp.float32)) * (1.0 + text_mod[:, 1]) + text_mod[:, 0]).astype(jnp.bfloat16)
    flat_rows = image_normed.reshape(IMG * R, D)
    queries = jnp.dot(flat_rows, qkv_weight[0], preferred_element_type=jnp.float32).reshape(IMG, R, H, HEAD)
    keys_img = jnp.dot(flat_rows, qkv_weight[1], preferred_element_type=jnp.float32).reshape(IMG, R, H, HEAD)
    values_img = jnp.dot(flat_rows, qkv_weight[2], preferred_element_type=jnp.float32).reshape(IMG, R, H, HEAD)
    queries = rounded(head_norm(queries, qk_gain[0]))
    keys_img = rounded(head_norm(keys_img, qk_gain[1]))
    values_img = rounded(values_img)
    keys_txt = jnp.dot(text_normed, text_weight[0], preferred_element_type=jnp.float32).reshape(TXT_ALL, H, HEAD)
    keys_txt = rounded(head_norm(keys_txt, qk_gain[1]))
    values_txt = rounded(jnp.dot(text_normed, text_weight[1], preferred_element_type=jnp.float32).reshape(TXT_ALL, H, HEAD))
    scale_factor = HEAD ** (-0.5)

    def attend(request):
        query_r = lax.dynamic_index_in_dim(queries, request, 1, keepdims=False)
        key_r = lax.dynamic_index_in_dim(keys_img, request, 1, keepdims=False)
        value_r = lax.dynamic_index_in_dim(values_img, request, 1, keepdims=False)
        image_scores = jnp.einsum('qhd,khd->hqk', query_r, key_r) * scale_factor
        text_scores = jnp.einsum('qhd,khd->hqk', query_r, keys_txt) * scale_factor
        allowed = segment_row == request
        text_scores = jnp.where(allowed[None, None, :], text_scores, masked_score)
        scores = jnp.concatenate([image_scores, text_scores], axis=2)
        row_max = lax.optimization_barrier(jnp.max(scores, axis=2, keepdims=True))
        weights = jnp.exp(scores - row_max)
        row_sum = lax.optimization_barrier(jnp.sum(weights, axis=2, keepdims=True))
        all_values = jnp.concatenate([value_r, values_txt], axis=0)
        mixed_heads = jnp.einsum('hqk,khd->hqd', rounded(weights), all_values) / row_sum
        return jnp.transpose(mixed_heads, (1, 0, 2)).astype(jnp.bfloat16)
    attended = lax.map(attend, jnp.arange(R, dtype=jnp.int32))
    attended = jnp.transpose(attended, (1, 0, 2, 3)).reshape(IMG * R, HD)
    group_cols = HD // N_WGT
    mixed = jnp.zeros((IMG * R, D), jnp.float32)
    for group in range(N_WGT):
        term = jnp.dot(attended[:, group * group_cols:(group + 1) * group_cols], out_weight[group * group_cols:(group + 1) * group_cols], preferred_element_type=jnp.float32)
        mixed = mixed + rounded(term)
    residual = hidden_f + modulate[:, 2] * mixed.reshape(IMG, R, D)
    branch_in = (layer_norm(residual) * (1.0 + modulate[:, 6]) + modulate[:, 5]).astype(jnp.bfloat16)
    expanded = jnp.dot(branch_in.reshape(IMG * R, D), expand_weight, preferred_element_type=jnp.float32)
    expanded = jax.nn.gelu(expanded, approximate=True).astype(jnp.bfloat16)
    unit_cols = FF // N_WGT
    branch = jnp.zeros((IMG * R, D), jnp.float32)
    for group in range(N_WGT):
        term = jnp.dot(expanded[:, group * unit_cols:(group + 1) * unit_cols], contract_weight[group * unit_cols:(group + 1) * unit_cols], preferred_element_type=jnp.float32)
        branch = branch + rounded(term)
    second = residual + modulate[:, 7] * branch.reshape(IMG, R, D)
    final_in = (layer_norm(second) * (1.0 + modulate[:, 9]) + modulate[:, 8]).astype(jnp.bfloat16)
    return jnp.dot(final_in.reshape(IMG * R, D), final_weight, preferred_element_type=jnp.float32).reshape(IMG, R, CH)

def reference(latent, img_hidden, txt_hidden, segments, timesteps, modulation, qk_gain, qkv_weight, text_weight, out_weight, expand_weight, contract_weight, final_weight):
    results = []
    for half_index in range(2):
        results.append(half_velocity(img_hidden[half_index], txt_hidden[half_index], segments[half_index], modulation[half_index], qk_gain, qkv_weight, text_weight, out_weight, expand_weight, contract_weight, final_weight))
    velocity = results[1] + guidance_scale * (results[0] - results[1])
    step_size = sigma_of(timesteps + 1) - sigma_of(timesteps)
    next_latent = latent + step_size[None, :, None] * velocity
    return (velocity, next_latent)
```

```python
import jax
import jax.numpy as jnp
from jax import lax
from jax.experimental import pallas as pl
from jax.experimental.pallas import tpu as pltpu
from jax.sharding import PartitionSpec as P

STEPS = 28


guidance_scale = 3.5
flow_shift = 3.0
eps_norm = 1e-06
masked_score = -1e30


def from_partner(value, axis, bit):
    mask = 2**bit
    pairs = [(source, source ^ mask) for source in range(lax.axis_size(axis))]
    return lax.ppermute(value, axis, pairs)


def layer_norm(values):
    center = jnp.mean(values, axis=-1, keepdims=True)
    centred = values - center
    spread = jnp.mean(centred * centred, axis=-1, keepdims=True)
    return centred * lax.rsqrt(spread + eps_norm)


def rows_by_rows(left, right):
    return lax.dot_general(
        left, right, (((1,), (1,)), ((), ())), preferred_element_type=jnp.float32
    )


def head_norm(values, gain_row):
    power = jnp.mean(values * values, axis=-1, keepdims=True)
    return values * lax.rsqrt(power + eps_norm) * gain_row


def sigma_of(index_row):
    time_left = 1.0 - index_row.astype(jnp.float32) / STEPS
    return flow_shift * time_left / (1.0 + (flow_shift - 1.0) * time_left)


def gather_kernel(count, seq_size, *refs):
    ins, outs = refs[:count], refs[count : 2 * count]
    z_send, z_recv, x_send, x_recv, c_send, c_recv, own_send, own_recv, local_sem = refs[2 * count :]
    span = seq_size // 2
    me, side = lax.axis_index("seq"), lax.axis_index("cfg")
    place, core = me // 2, me % 2
    partner_core = me + 1 - 2 * core

    def half_lanes(ref, half):
        width = ref.shape[-1] // 2
        return pl.ds(pl.multiple_of(half * width, 128), width)

    def shard(item, index, half=None):
        rows = ins[item].shape[1]
        at_rows = pl.ds(pl.multiple_of(index * rows, 16), rows)
        if half is None:
            return outs[item].at[:, at_rows, :]
        return outs[item].at[:, at_rows, half_lanes(outs[item], half)]

    def origin(way, dist):
        return me - 2 * dist if way == 0 else me + 2 * dist

    def exists(way, dist):
        return place - dist >= 0 if way == 0 else place + dist < span

    def hop(item, way, dist):
        if dist == 0:
            source = ins[item].at[:, :, half_lanes(ins[item], side)]
        else:
            source = shard(item, origin(way, dist), side)
        return pltpu.make_async_remote_copy(
            src_ref=source,
            dst_ref=shard(item, origin(way, dist), side),
            send_sem=z_send.at[item, way, dist],
            recv_sem=z_recv.at[item, way, dist],
            device_id={"seq": me + 2 if way == 0 else me - 2},
            device_id_type=pl.DeviceIdType.MESH,
        )

    def landed(item, way, dist):
        here = shard(item, origin(way, dist), side)
        return pltpu.make_async_remote_copy(
            src_ref=here,
            dst_ref=here,
            send_sem=z_send.at[item, way, dist - 1],
            recv_sem=z_recv.at[item, way, dist - 1],
            device_id={"cfg": 1 - side},
            device_id_type=pl.DeviceIdType.MESH,
        )

    def across(item, way, dist, half):
        here = shard(item, origin(way, dist), half)
        return pltpu.make_async_remote_copy(
            src_ref=here,
            dst_ref=here,
            send_sem=x_send.at[item, way, dist],
            recv_sem=x_recv.at[item, way, dist],
            device_id={"cfg": 1 - side},
            device_id_type=pl.DeviceIdType.MESH,
        )

    def to_core(item, way, dist, home):
        here = shard(item, origin(way, dist) - me + home)
        return pltpu.make_async_remote_copy(
            src_ref=here,
            dst_ref=here,
            send_sem=c_send.at[item, way, dist],
            recv_sem=c_recv.at[item, way, dist],
            device_id={"seq": partner_core},
            device_id_type=pl.DeviceIdType.MESH,
        )

    def own_to_core(item, home):
        return pltpu.make_async_remote_copy(
            src_ref=ins[item],
            dst_ref=shard(item, home),
            send_sem=own_send.at[item],
            recv_sem=own_recv.at[item],
            device_id={"seq": partner_core},
            device_id_type=pl.DeviceIdType.MESH,
        )

    def local(item):
        return pltpu.make_async_copy(ins[item], shard(item, me), local_sem.at[item])

    barrier = pltpu.get_barrier_semaphore()
    pl.semaphore_signal(barrier, device_id={"cfg": 1 - side}, device_id_type=pl.DeviceIdType.MESH)
    pl.semaphore_signal(barrier, device_id={"seq": partner_core}, device_id_type=pl.DeviceIdType.MESH)
    for way in (0, 1):

        @pl.when(exists(1 - way, 1))
        def _():
            pl.semaphore_signal(
                barrier,
                device_id={"seq": me + 2 if way == 0 else me - 2},
                device_id_type=pl.DeviceIdType.MESH,
            )

    peers = 2 + lax.min(place, 1) + lax.min(span - 1 - place, 1)
    pl.semaphore_wait(barrier, peers)

    for item in range(count):
        for way in (0, 1):

            @pl.when(exists(1 - way, 1))
            def _():
                hop(item, way, 0).start()

    for item in range(count):
        own_to_core(item, me).start()
        local(item).start()

    def pass_to_core(item, dist):
        for way in (0, 1):

            @pl.when(exists(way, dist))
            def _():
                across(item, way, dist, 1 - side).wait_recv()
                to_core(item, way, dist, me).start()

    for dist in range(1, span):
        for item in range(count):
            for way in (0, 1):

                @pl.when(exists(way, dist))
                def _():
                    landed(item, way, dist).wait_recv()

                    @pl.when(exists(1 - way, 1))
                    def _():
                        hop(item, way, dist).start()

                    across(item, way, dist, side).start()

            if dist > 1:
                pass_to_core(item, dist - 1)
    for item in range(count):
        pass_to_core(item, span - 1)

    for item in range(count):
        own_to_core(item, partner_core).wait_recv()
        own_to_core(item, me).wait_send()
        local(item).wait()
        for way in (0, 1):

            @pl.when(exists(1 - way, 1))
            def _():
                hop(item, way, 0).wait_send()

            for dist in range(1, span):

                @pl.when(exists(way, dist))
                def _():
                    @pl.when(exists(1 - way, 1))
                    def _():
                        hop(item, way, dist).wait_send()

                    across(item, way, dist, side).wait_send()
                    to_core(item, way, dist, me).wait_send()
                    to_core(item, way, dist, partner_core).wait_recv()


def gather_rows(arrays, collective_id):
    seq_size = lax.axis_size("seq")
    fits = lax.axis_size("cfg") == 2 and seq_size <= 8 and seq_size % 2 == 0
    for array in arrays:
        fits = fits and array.shape[1] % 16 == 0 and array.shape[2] % 256 == 0
    if not fits:
        return [lax.all_gather(array, "seq", axis=1, tiled=True) for array in arrays]
    count, span = len(arrays), seq_size // 2
    dma = pltpu.SemaphoreType.DMA
    whole = [(a.shape[0], a.shape[1] * seq_size, a.shape[2]) for a in arrays]
    moved = sum(2 * a.size * seq_size for a in arrays)
    return pl.pallas_call(
        lambda *refs: gather_kernel(count, seq_size, *refs),
        out_shape=[jax.ShapeDtypeStruct(s, jnp.bfloat16) for s in whole],
        in_specs=[pl.BlockSpec(memory_space=pl.ANY)] * count,
        out_specs=[pl.BlockSpec(memory_space=pl.ANY)] * count,
        scratch_shapes=[dma((count, 2, span))] * 6 + [dma((count,))] * 3,
        compiler_params=pltpu.CompilerParams(
            collective_id=collective_id, has_side_effects=True
        ),
        cost_estimate=pl.CostEstimate(flops=0, bytes_accessed=2 * moved, transcendentals=0),
        name="gather_rows",
    )(*arrays)


def body(
    latent,
    img_hidden,
    txt_hidden,
    segments,
    timesteps,
    modulation,
    qk_gain,
    qkv_weight,
    text_weight,
    out_weight,
    expand_weight,
    contract_weight,
    final_weight,
):
    tokens_here = img_hidden.shape[1]
    requests = img_hidden.shape[2]
    feat_width = img_hidden.shape[3]
    head_size = qk_gain.shape[1]
    local_cols = qkv_weight.shape[2]
    heads_here = local_cols // head_size
    text_here = txt_hidden.shape[1]
    modulate = modulation[0]
    hidden = img_hidden[0].astype(jnp.float32)
    image_normed = (layer_norm(hidden) * (1.0 + modulate[:, 1]) + modulate[:, 0]).astype(
        jnp.bfloat16
    )
    row_count = tokens_here * requests
    token_rows = image_normed.reshape(row_count, feat_width)
    segment_row = segments[0]
    one_hot = (segment_row[:, None] == jnp.arange(requests, dtype=jnp.int32)[None, :]).astype(
        jnp.float32
    )
    text_mod = jnp.einsum("tr,rkd->tkd", one_hot, modulate[:, 3:5], precision=lax.Precision.HIGHEST)
    text_normed = (
        layer_norm(txt_hidden[0].astype(jnp.float32)) * (1.0 + text_mod[:, 1]) + text_mod[:, 0]
    ).astype(jnp.bfloat16)
    qkv_full, text_full, out_full, contract_full, expand_full = gather_rows(
        [
            qkv_weight,
            text_weight,
            out_weight.T[None],
            contract_weight.T[None],
            expand_weight[None],
        ],
        0,
    )
    image_term = jnp.einsum(
        "rd,kdc->rkc", token_rows, qkv_full, preferred_element_type=jnp.float32
    )
    text_term = jnp.einsum(
        "rd,kdc->rkc", text_normed, text_full, preferred_element_type=jnp.float32
    )
    queries = head_norm(
        image_term[:, 0].reshape(tokens_here, requests, heads_here, head_size), qk_gain[0]
    ).astype(jnp.bfloat16)
    keys_img = head_norm(
        image_term[:, 1].reshape(tokens_here, requests, heads_here, head_size), qk_gain[1]
    ).astype(jnp.bfloat16)
    values_img = image_term[:, 2].reshape(tokens_here, requests, local_cols).astype(jnp.bfloat16)
    keys_txt = head_norm(
        text_term[:, 0].reshape(text_here, heads_here, head_size), qk_gain[1]
    ).astype(jnp.bfloat16)
    values_txt = text_term[:, 1].astype(jnp.bfloat16)
    image_pair = jnp.stack(
        [keys_img.reshape(tokens_here, requests, local_cols), values_img], axis=2
    )
    text_pair = jnp.stack([keys_txt.reshape(text_here, local_cols), values_txt], axis=1)
    text_owner = segment_row.astype(jnp.float32).astype(jnp.bfloat16)
    scale_factor = head_size ** (-0.5)
    request_ids = jnp.arange(requests, dtype=jnp.float32)
    running_max = jnp.full((requests, heads_here, tokens_here), masked_score, jnp.float32)
    pair_cols = 2 * local_cols
    owner_row = jnp.pad(text_owner, (0, pair_cols - text_here))[None]
    packed = jnp.concatenate(
        [
            image_pair.reshape(row_count, pair_cols),
            text_pair.reshape(text_here, pair_cols),
            owner_row,
        ],
        axis=0,
    )
    gathered = lax.all_gather(packed, "seq", axis=0)
    image_piece = gathered[:, :row_count].reshape(-1, requests, 2, local_cols)
    text_piece = gathered[:, row_count : row_count + text_here].reshape(-1, 2, local_cols)
    owner_piece = gathered[:, row_count + text_here, :text_here].reshape(-1)
    piece_keys = image_piece[:, :, 0].reshape(-1, requests, heads_here, head_size)
    piece_values = image_piece[:, :, 1].reshape(-1, requests, heads_here, head_size)
    text_keys = text_piece[:, 0].reshape(-1, heads_here, head_size)
    text_values = text_piece[:, 1].reshape(-1, heads_here, head_size)
    image_scores = (
        jnp.einsum("qrhd,krhd->rhqk", queries, piece_keys, preferred_element_type=jnp.float32)
        * scale_factor
    )
    text_scores = (
        jnp.einsum("qrhd,khd->rhqk", queries, text_keys, preferred_element_type=jnp.float32)
        * scale_factor
    )
    allowed = owner_piece.astype(jnp.float32)[None, :] == request_ids[:, None]
    text_scores = jnp.where(allowed[:, None, None, :], text_scores, masked_score)
    block_max = jnp.maximum(jnp.max(image_scores, axis=-1), jnp.max(text_scores, axis=-1))
    new_max = jnp.maximum(running_max, block_max)
    image_weights = jnp.exp(image_scores - new_max[..., None])
    text_weights = jnp.exp(text_scores - new_max[..., None])
    new_sum = jnp.sum(image_weights, axis=-1) + jnp.sum(text_weights, axis=-1)
    new_acc = jnp.einsum(
        "rhqk,krhd->rhqd",
        image_weights.astype(jnp.bfloat16),
        piece_values,
        preferred_element_type=jnp.float32,
    )
    new_acc = new_acc + jnp.einsum(
        "rhqk,khd->rhqd",
        text_weights.astype(jnp.bfloat16),
        text_values,
        preferred_element_type=jnp.float32,
    )
    attended = new_acc / new_sum[..., None]
    attended = (
        jnp.transpose(attended, (2, 0, 1, 3)).reshape(row_count, local_cols).astype(jnp.bfloat16)
    )
    share_rows = row_count // lax.axis_size("wgt")
    piece_rows = attended
    mixed = lax.psum_scatter(
        rows_by_rows(piece_rows, out_full[0]).astype(jnp.bfloat16),
        "wgt",
        scatter_dimension=0,
        tiled=True,
    ).astype(jnp.float32)
    tokens_out = share_rows // requests
    row_place = lax.axis_index("wgt") * share_rows
    base_rows = lax.dynamic_slice_in_dim(
        hidden.reshape(row_count, feat_width), row_place, share_rows, 0
    )
    residual = base_rows.reshape(tokens_out, requests, feat_width) + modulate[:, 2] * mixed.reshape(
        tokens_out, requests, feat_width
    )
    branch_in = (layer_norm(residual) * (1.0 + modulate[:, 6]) + modulate[:, 5]).astype(
        jnp.bfloat16
    )
    branch_rows = lax.all_gather(
        branch_in.reshape(share_rows, feat_width), "wgt", axis=0, tiled=True
    )
    expanded = jnp.dot(
        branch_rows,
        expand_full[0],
        preferred_element_type=jnp.float32,
    )
    expanded = jax.nn.gelu(expanded, approximate=True).astype(jnp.bfloat16)
    piece_rows = expanded
    branch = lax.psum_scatter(
        rows_by_rows(piece_rows, contract_full[0]).astype(jnp.bfloat16),
        "wgt",
        scatter_dimension=0,
        tiled=True,
    ).astype(jnp.float32)
    second = residual + modulate[:, 7] * branch.reshape(tokens_out, requests, feat_width)
    final_in = (layer_norm(second) * (1.0 + modulate[:, 9]) + modulate[:, 8]).astype(jnp.bfloat16)
    own_velocity = jnp.dot(
        final_in.reshape(share_rows, feat_width), final_weight, preferred_element_type=jnp.float32
    ).reshape(tokens_out, requests, -1)
    guide_side = lax.axis_index("cfg")
    guided_count = latent.shape[1]
    kept_rows = lax.dynamic_slice_in_dim(own_velocity, guide_side * guided_count, guided_count, 1)
    sent_rows = lax.dynamic_slice_in_dim(
        own_velocity, (1 - guide_side) * guided_count, guided_count, 1
    )
    partner_velocity = from_partner(sent_rows, "cfg", 0)
    is_first = guide_side == 0
    conditional = jnp.where(is_first, kept_rows, partner_velocity)
    unconditional = jnp.where(is_first, partner_velocity, kept_rows)
    velocity = unconditional + guidance_scale * (conditional - unconditional)
    step_size = sigma_of(timesteps + 1) - sigma_of(timesteps)
    step_here = lax.dynamic_slice_in_dim(step_size, guide_side * guided_count, guided_count, 0)
    next_latent = latent + step_here[None, :, None] * velocity
    return (velocity, next_latent)


def solution(mesh):
    return jax.shard_map(
        body,
        mesh=mesh,
        in_specs=(
            P(("seq", "wgt"), "cfg", None),
            P("cfg", "seq", None, None),
            P("cfg", "seq", None),
            P("cfg", "seq"),
            P(),
            P("cfg", None, None, None),
            P(),
            P(None, "seq", "wgt"),
            P(None, "seq", "wgt"),
            P("wgt", "seq"),
            P("seq", "wgt"),
            P("wgt", "seq"),
            P(),
        ),
        out_specs=(P(("seq", "wgt"), "cfg", None), P(("seq", "wgt"), "cfg", None)),
        check_vma=False,
    )
```

```python
import jax
import jax.numpy as jnp
from jax import lax
from jax.experimental import pallas as pl
from jax.experimental.pallas import tpu as pltpu
from jax.sharding import PartitionSpec as P

STEPS = 28


guidance_scale = 3.5
flow_shift = 3.0
eps_norm = 1e-06
masked_score = -1e30


def from_partner(value, axis, bit):
    mask = 2**bit
    pairs = [(source, source ^ mask) for source in range(lax.axis_size(axis))]
    return lax.ppermute(value, axis, pairs)


def layer_norm(values):
    center = jnp.mean(values, axis=-1, keepdims=True)
    centred = values - center
    spread = jnp.mean(centred * centred, axis=-1, keepdims=True)
    return centred * lax.rsqrt(spread + eps_norm)


def rows_by_rows(left, right):
    return lax.dot_general(
        left, right, (((1,), (1,)), ((), ())), preferred_element_type=jnp.float32
    )


def head_norm(values, gain_row):
    power = jnp.mean(values * values, axis=-1, keepdims=True)
    return values * lax.rsqrt(power + eps_norm) * gain_row


def sigma_of(index_row):
    time_left = 1.0 - index_row.astype(jnp.float32) / STEPS
    return flow_shift * time_left / (1.0 + (flow_shift - 1.0) * time_left)


def gather_kernel(count, seq_size, *refs):
    ins, outs = refs[:count], refs[count : 2 * count]
    z_send, z_recv, x_send, x_recv, c_send, c_recv, own_send, own_recv, local_sem = refs[2 * count :]
    span = seq_size // 2
    me, side = lax.axis_index("seq"), lax.axis_index("cfg")
    place, core = me // 2, me % 2
    partner_core = me + 1 - 2 * core

    def half_lanes(ref, half):
        width = ref.shape[-1] // 2
        return pl.ds(pl.multiple_of(half * width, 128), width)

    def shard(item, index, half=None):
        rows = ins[item].shape[1]
        at_rows = pl.ds(pl.multiple_of(index * rows, 16), rows)
        if half is None:
            return outs[item].at[:, at_rows, :]
        return outs[item].at[:, at_rows, half_lanes(outs[item], half)]

    def origin(way, dist):
        return me - 2 * dist if way == 0 else me + 2 * dist

    def exists(way, dist):
        return place - dist >= 0 if way == 0 else place + dist < span

    def hop(item, way, dist):
        if dist == 0:
            source = ins[item].at[:, :, half_lanes(ins[item], side)]
        else:
            source = shard(item, origin(way, dist), side)
        return pltpu.make_async_remote_copy(
            src_ref=source,
            dst_ref=shard(item, origin(way, dist), side),
            send_sem=z_send.at[item, way, dist],
            recv_sem=z_recv.at[item, way, dist],
            device_id={"seq": me + 2 if way == 0 else me - 2},
            device_id_type=pl.DeviceIdType.MESH,
        )

    def landed(item, way, dist):
        here = shard(item, origin(way, dist), side)
        return pltpu.make_async_remote_copy(
            src_ref=here,
            dst_ref=here,
            send_sem=z_send.at[item, way, dist - 1],
            recv_sem=z_recv.at[item, way, dist - 1],
            device_id={"cfg": 1 - side},
            device_id_type=pl.DeviceIdType.MESH,
        )

    def across(item, way, dist, half):
        here = shard(item, origin(way, dist), half)
        return pltpu.make_async_remote_copy(
            src_ref=here,
            dst_ref=here,
            send_sem=x_send.at[item, way, dist],
            recv_sem=x_recv.at[item, way, dist],
            device_id={"cfg": 1 - side},
            device_id_type=pl.DeviceIdType.MESH,
        )

    def to_core(item, way, dist, home):
        here = shard(item, origin(way, dist) - me + home)
        return pltpu.make_async_remote_copy(
            src_ref=here,
            dst_ref=here,
            send_sem=c_send.at[item, way, dist],
            recv_sem=c_recv.at[item, way, dist],
            device_id={"seq": partner_core},
            device_id_type=pl.DeviceIdType.MESH,
        )

    def own_to_core(item, home):
        return pltpu.make_async_remote_copy(
            src_ref=ins[item],
            dst_ref=shard(item, home),
            send_sem=own_send.at[item],
            recv_sem=own_recv.at[item],
            device_id={"seq": partner_core},
            device_id_type=pl.DeviceIdType.MESH,
        )

    def local(item):
        return pltpu.make_async_copy(ins[item], shard(item, me), local_sem.at[item])

    barrier = pltpu.get_barrier_semaphore()
    pl.semaphore_signal(barrier, device_id={"cfg": 1 - side}, device_id_type=pl.DeviceIdType.MESH)
    pl.semaphore_signal(barrier, device_id={"seq": partner_core}, device_id_type=pl.DeviceIdType.MESH)
    for way in (0, 1):

        @pl.when(exists(1 - way, 1))
        def _():
            pl.semaphore_signal(
                barrier,
                device_id={"seq": me + 2 if way == 0 else me - 2},
                device_id_type=pl.DeviceIdType.MESH,
            )

    peers = 2 + lax.min(place, 1) + lax.min(span - 1 - place, 1)
    pl.semaphore_wait(barrier, peers)

    for item in range(count):
        for way in (0, 1):

            @pl.when(exists(1 - way, 1))
            def _():
                hop(item, way, 0).start()

    for item in range(count):
        own_to_core(item, me).start()
        local(item).start()

    def pass_to_core(item, dist):
        for way in (0, 1):

            @pl.when(exists(way, dist))
            def _():
                across(item, way, dist, 1 - side).wait_recv()
                to_core(item, way, dist, me).start()

    for dist in range(1, span):
        for item in range(count):
            for way in (0, 1):

                @pl.when(exists(way, dist))
                def _():
                    landed(item, way, dist).wait_recv()

                    @pl.when(exists(1 - way, 1))
                    def _():
                        hop(item, way, dist).start()

                    across(item, way, dist, side).start()

            if dist > 1:
                pass_to_core(item, dist - 1)
    for item in range(count):
        pass_to_core(item, span - 1)

    for item in range(count):
        own_to_core(item, partner_core).wait_recv()
        own_to_core(item, me).wait_send()
        local(item).wait()
        for way in (0, 1):

            @pl.when(exists(1 - way, 1))
            def _():
                hop(item, way, 0).wait_send()

            for dist in range(1, span):

                @pl.when(exists(way, dist))
                def _():
                    @pl.when(exists(1 - way, 1))
                    def _():
                        hop(item, way, dist).wait_send()

                    across(item, way, dist, side).wait_send()
                    to_core(item, way, dist, me).wait_send()
                    to_core(item, way, dist, partner_core).wait_recv()


def gather_rows(arrays, collective_id):
    seq_size = lax.axis_size("seq")
    fits = lax.axis_size("cfg") == 2 and seq_size <= 8 and seq_size % 2 == 0
    for array in arrays:
        fits = fits and array.shape[1] % 16 == 0 and array.shape[2] % 256 == 0
    if not fits:
        return [lax.all_gather(array, "seq", axis=1, tiled=True) for array in arrays]
    count, span = len(arrays), seq_size // 2
    dma = pltpu.SemaphoreType.DMA
    whole = [(a.shape[0], a.shape[1] * seq_size, a.shape[2]) for a in arrays]
    moved = sum(2 * a.size * seq_size for a in arrays)
    return pl.pallas_call(
        lambda *refs: gather_kernel(count, seq_size, *refs),
        out_shape=[jax.ShapeDtypeStruct(s, jnp.bfloat16) for s in whole],
        in_specs=[pl.BlockSpec(memory_space=pl.ANY)] * count,
        out_specs=[pl.BlockSpec(memory_space=pl.ANY)] * count,
        scratch_shapes=[dma((count, 2, span))] * 6 + [dma((count,))] * 3,
        compiler_params=pltpu.CompilerParams(
            collective_id=collective_id, has_side_effects=True
        ),
        cost_estimate=pl.CostEstimate(flops=0, bytes_accessed=2 * moved, transcendentals=0),
        name="gather_rows",
    )(*arrays)


def body(
    latent,
    img_hidden,
    txt_hidden,
    segments,
    timesteps,
    modulation,
    qk_gain,
    qkv_weight,
    text_weight,
    out_weight,
    expand_weight,
    contract_weight,
    final_weight,
):
    tokens_here = img_hidden.shape[1]
    requests = img_hidden.shape[2]
    feat_width = img_hidden.shape[3]
    head_size = qk_gain.shape[1]
    local_cols = qkv_weight.shape[2]
    heads_here = local_cols // head_size
    text_here = txt_hidden.shape[1]
    modulate = modulation[0]
    hidden = img_hidden[0].astype(jnp.float32)
    image_normed = (layer_norm(hidden) * (1.0 + modulate[:, 1]) + modulate[:, 0]).astype(
        jnp.bfloat16
    )
    row_count = tokens_here * requests
    token_rows = image_normed.reshape(row_count, feat_width)
    segment_row = segments[0]
    one_hot = (segment_row[:, None] == jnp.arange(requests, dtype=jnp.int32)[None, :]).astype(
        jnp.float32
    )
    text_mod = jnp.einsum("tr,rkd->tkd", one_hot, modulate[:, 3:5], precision=lax.Precision.HIGHEST)
    text_normed = (
        layer_norm(txt_hidden[0].astype(jnp.float32)) * (1.0 + text_mod[:, 1]) + text_mod[:, 0]
    ).astype(jnp.bfloat16)
    owner_piece = lax.all_gather(
        segments[0].astype(jnp.float32).astype(jnp.bfloat16), "seq", axis=0, tiled=True
    )
    qkv_full, text_full = gather_rows([qkv_weight, text_weight], 0)
    image_term = jnp.einsum(
        "rd,kdc->rkc", token_rows, qkv_full, preferred_element_type=jnp.float32
    )
    text_term = jnp.einsum(
        "rd,kdc->rkc", text_normed, text_full, preferred_element_type=jnp.float32
    )
    queries = head_norm(
        image_term[:, 0].reshape(tokens_here, requests, heads_here, head_size), qk_gain[0]
    ).astype(jnp.bfloat16)
    keys_img = head_norm(
        image_term[:, 1].reshape(tokens_here, requests, heads_here, head_size), qk_gain[1]
    ).astype(jnp.bfloat16)
    values_img = image_term[:, 2].reshape(tokens_here, requests, local_cols).astype(jnp.bfloat16)
    keys_txt = head_norm(
        text_term[:, 0].reshape(text_here, heads_here, head_size), qk_gain[1]
    ).astype(jnp.bfloat16)
    values_txt = text_term[:, 1].astype(jnp.bfloat16)
    image_pair = jnp.stack(
        [keys_img.reshape(tokens_here, requests, local_cols), values_img], axis=2
    )
    text_pair = jnp.stack([keys_txt.reshape(text_here, local_cols), values_txt], axis=1)
    scale_factor = head_size ** (-0.5)
    request_ids = jnp.arange(requests, dtype=jnp.float32)
    running_max = jnp.full((requests, heads_here, tokens_here), masked_score, jnp.float32)
    image_piece = lax.all_gather(image_pair, "seq", axis=0, tiled=True)
    text_piece = lax.all_gather(text_pair, "seq", axis=0, tiled=True)
    late_weights, _ = lax.optimization_barrier(
        ((out_weight, contract_weight, expand_weight), image_pair)
    )
    late_full = gather_rows(
        [late_weights[0].T[None], late_weights[1].T[None], late_weights[2][None]], 1
    )
    (out_full, contract_full, expand_full), queries = lax.optimization_barrier(
        (tuple(late_full), queries)
    )
    piece_keys = image_piece[:, :, 0].reshape(-1, requests, heads_here, head_size)
    piece_values = image_piece[:, :, 1].reshape(-1, requests, heads_here, head_size)
    text_keys = text_piece[:, 0].reshape(-1, heads_here, head_size)
    text_values = text_piece[:, 1].reshape(-1, heads_here, head_size)
    image_scores = (
        jnp.einsum("qrhd,krhd->rhqk", queries, piece_keys, preferred_element_type=jnp.float32)
        * scale_factor
    )
    text_scores = (
        jnp.einsum("qrhd,khd->rhqk", queries, text_keys, preferred_element_type=jnp.float32)
        * scale_factor
    )
    allowed = owner_piece.astype(jnp.float32)[None, :] == request_ids[:, None]
    text_scores = jnp.where(allowed[:, None, None, :], text_scores, masked_score)
    block_max = jnp.maximum(jnp.max(image_scores, axis=-1), jnp.max(text_scores, axis=-1))
    new_max = jnp.maximum(running_max, block_max)
    image_weights = jnp.exp(image_scores - new_max[..., None])
    text_weights = jnp.exp(text_scores - new_max[..., None])
    new_sum = jnp.sum(image_weights, axis=-1) + jnp.sum(text_weights, axis=-1)
    new_acc = jnp.einsum(
        "rhqk,krhd->rhqd",
        image_weights.astype(jnp.bfloat16),
        piece_values,
        preferred_element_type=jnp.float32,
    )
    new_acc = new_acc + jnp.einsum(
        "rhqk,khd->rhqd",
        text_weights.astype(jnp.bfloat16),
        text_values,
        preferred_element_type=jnp.float32,
    )
    attended = new_acc / new_sum[..., None]
    attended = (
        jnp.transpose(attended, (2, 0, 1, 3)).reshape(row_count, local_cols).astype(jnp.bfloat16)
    )
    share_rows = row_count // lax.axis_size("wgt")
    piece_rows = attended
    mixed = lax.psum_scatter(
        rows_by_rows(piece_rows, out_full[0]).astype(jnp.bfloat16),
        "wgt",
        scatter_dimension=0,
        tiled=True,
    ).astype(jnp.float32)
    tokens_out = share_rows // requests
    row_place = lax.axis_index("wgt") * share_rows
    base_rows = lax.dynamic_slice_in_dim(
        hidden.reshape(row_count, feat_width), row_place, share_rows, 0
    )
    residual = base_rows.reshape(tokens_out, requests, feat_width) + modulate[:, 2] * mixed.reshape(
        tokens_out, requests, feat_width
    )
    branch_in = (layer_norm(residual) * (1.0 + modulate[:, 6]) + modulate[:, 5]).astype(
        jnp.bfloat16
    )
    branch_rows = lax.all_gather(
        branch_in.reshape(share_rows, feat_width), "wgt", axis=0, tiled=True
    )
    expanded = jnp.dot(
        branch_rows,
        expand_full[0],
        preferred_element_type=jnp.float32,
    )
    expanded = jax.nn.gelu(expanded, approximate=True).astype(jnp.bfloat16)
    piece_rows = expanded
    branch = lax.psum_scatter(
        rows_by_rows(piece_rows, contract_full[0]).astype(jnp.bfloat16),
        "wgt",
        scatter_dimension=0,
        tiled=True,
    ).astype(jnp.float32)
    second = residual + modulate[:, 7] * branch.reshape(tokens_out, requests, feat_width)
    final_in = (layer_norm(second) * (1.0 + modulate[:, 9]) + modulate[:, 8]).astype(jnp.bfloat16)
    own_velocity = jnp.dot(
        final_in.reshape(share_rows, feat_width), final_weight, preferred_element_type=jnp.float32
    ).reshape(tokens_out, requests, -1)
    guide_side = lax.axis_index("cfg")
    guided_count = latent.shape[1]
    kept_rows = lax.dynamic_slice_in_dim(own_velocity, guide_side * guided_count, guided_count, 1)
    sent_rows = lax.dynamic_slice_in_dim(
        own_velocity, (1 - guide_side) * guided_count, guided_count, 1
    )
    partner_velocity = from_partner(sent_rows, "cfg", 0)
    is_first = guide_side == 0
    conditional = jnp.where(is_first, kept_rows, partner_velocity)
    unconditional = jnp.where(is_first, partner_velocity, kept_rows)
    velocity = unconditional + guidance_scale * (conditional - unconditional)
    step_size = sigma_of(timesteps + 1) - sigma_of(timesteps)
    step_here = lax.dynamic_slice_in_dim(step_size, guide_side * guided_count, guided_count, 0)
    next_latent = latent + step_here[None, :, None] * velocity
    return (velocity, next_latent)


def solution(mesh):
    return jax.shard_map(
        body,
        mesh=mesh,
        in_specs=(
            P(("seq", "wgt"), "cfg", None),
            P("cfg", "seq", None, None),
            P("cfg", "seq", None),
            P("cfg", "seq"),
            P(),
            P("cfg", None, None, None),
            P(),
            P(None, "seq", "wgt"),
            P(None, "seq", "wgt"),
            P("wgt", "seq"),
            P("seq", "wgt"),
            P("wgt", "seq"),
            P(),
        ),
        out_specs=(P(("seq", "wgt"), "cfg", None), P(("seq", "wgt"), "cfg", None)),
        check_vma=False,
    )
```

```python
import jax
import jax.numpy as jnp
from jax import lax
from jax.experimental import pallas as pl
from jax.experimental.pallas import tpu as pltpu
from jax.sharding import PartitionSpec as P

STEPS = 28


guidance_scale = 3.5
flow_shift = 3.0
eps_norm = 1e-06
masked_score = -1e30


def from_partner(value, axis, bit):
    mask = 2**bit
    pairs = [(source, source ^ mask) for source in range(lax.axis_size(axis))]
    return lax.ppermute(value, axis, pairs)


def layer_norm(values):
    center = jnp.mean(values, axis=-1, keepdims=True)
    centred = values - center
    spread = jnp.mean(centred * centred, axis=-1, keepdims=True)
    return centred * lax.rsqrt(spread + eps_norm)


def rows_by_rows(left, right):
    return lax.dot_general(
        left, right, (((1,), (1,)), ((), ())), preferred_element_type=jnp.float32
    )


def head_norm(values, gain_row):
    power = jnp.mean(values * values, axis=-1, keepdims=True)
    return values * lax.rsqrt(power + eps_norm) * gain_row


def sigma_of(index_row):
    time_left = 1.0 - index_row.astype(jnp.float32) / STEPS
    return flow_shift * time_left / (1.0 + (flow_shift - 1.0) * time_left)


def gather_kernel(count, seq_size, *refs):
    ins, outs = refs[:count], refs[count : 2 * count]
    z_send, z_recv, x_send, x_recv, c_send, c_recv, own_send, own_recv, local_sem = refs[2 * count :]
    span = seq_size // 2
    me, side = lax.axis_index("seq"), lax.axis_index("cfg")
    place, core = me // 2, me % 2
    partner_core = me + 1 - 2 * core

    def half_lanes(ref, half):
        width = ref.shape[-1] // 2
        return pl.ds(pl.multiple_of(half * width, 128), width)

    def shard(item, index, half=None):
        rows = ins[item].shape[1]
        at_rows = pl.ds(pl.multiple_of(index * rows, 16), rows)
        if half is None:
            return outs[item].at[:, at_rows, :]
        return outs[item].at[:, at_rows, half_lanes(outs[item], half)]

    def origin(way, dist):
        return me - 2 * dist if way == 0 else me + 2 * dist

    def exists(way, dist):
        return place - dist >= 0 if way == 0 else place + dist < span

    def hop(item, way, dist):
        if dist == 0:
            source = ins[item].at[:, :, half_lanes(ins[item], side)]
        else:
            source = shard(item, origin(way, dist), side)
        return pltpu.make_async_remote_copy(
            src_ref=source,
            dst_ref=shard(item, origin(way, dist), side),
            send_sem=z_send.at[item, way, dist],
            recv_sem=z_recv.at[item, way, dist],
            device_id={"seq": me + 2 if way == 0 else me - 2},
            device_id_type=pl.DeviceIdType.MESH,
        )

    def landed(item, way, dist):
        here = shard(item, origin(way, dist), side)
        return pltpu.make_async_remote_copy(
            src_ref=here,
            dst_ref=here,
            send_sem=z_send.at[item, way, dist - 1],
            recv_sem=z_recv.at[item, way, dist - 1],
            device_id={"cfg": 1 - side},
            device_id_type=pl.DeviceIdType.MESH,
        )

    def across(item, way, dist, half):
        here = shard(item, origin(way, dist), half)
        return pltpu.make_async_remote_copy(
            src_ref=here,
            dst_ref=here,
            send_sem=x_send.at[item, way, dist],
            recv_sem=x_recv.at[item, way, dist],
            device_id={"cfg": 1 - side},
            device_id_type=pl.DeviceIdType.MESH,
        )

    def to_core(item, way, dist, home):
        here = shard(item, origin(way, dist) - me + home)
        return pltpu.make_async_remote_copy(
            src_ref=here,
            dst_ref=here,
            send_sem=c_send.at[item, way, dist],
            recv_sem=c_recv.at[item, way, dist],
            device_id={"seq": partner_core},
            device_id_type=pl.DeviceIdType.MESH,
        )

    def own_to_core(item, home):
        return pltpu.make_async_remote_copy(
            src_ref=ins[item],
            dst_ref=shard(item, home),
            send_sem=own_send.at[item],
            recv_sem=own_recv.at[item],
            device_id={"seq": partner_core},
            device_id_type=pl.DeviceIdType.MESH,
        )

    def local(item):
        return pltpu.make_async_copy(ins[item], shard(item, me), local_sem.at[item])

    barrier = pltpu.get_barrier_semaphore()
    pl.semaphore_signal(barrier, device_id={"cfg": 1 - side}, device_id_type=pl.DeviceIdType.MESH)
    pl.semaphore_signal(barrier, device_id={"seq": partner_core}, device_id_type=pl.DeviceIdType.MESH)
    for way in (0, 1):

        @pl.when(exists(1 - way, 1))
        def _():
            pl.semaphore_signal(
                barrier,
                device_id={"seq": me + 2 if way == 0 else me - 2},
                device_id_type=pl.DeviceIdType.MESH,
            )

    peers = 2 + lax.min(place, 1) + lax.min(span - 1 - place, 1)
    pl.semaphore_wait(barrier, peers)

    for item in range(count):
        for way in (0, 1):

            @pl.when(exists(1 - way, 1))
            def _():
                hop(item, way, 0).start()

    for item in range(count):
        own_to_core(item, me).start()
        local(item).start()

    def pass_to_core(item, dist):
        for way in (0, 1):

            @pl.when(exists(way, dist))
            def _():
                across(item, way, dist, 1 - side).wait_recv()
                to_core(item, way, dist, me).start()

    for dist in range(1, span):
        for item in range(count):
            for way in (0, 1):

                @pl.when(exists(way, dist))
                def _():
                    landed(item, way, dist).wait_recv()

                    @pl.when(exists(1 - way, 1))
                    def _():
                        hop(item, way, dist).start()

                    across(item, way, dist, side).start()

            if dist > 1:
                pass_to_core(item, dist - 1)
    for item in range(count):
        pass_to_core(item, span - 1)

    for item in range(count):
        own_to_core(item, partner_core).wait_recv()
        own_to_core(item, me).wait_send()
        local(item).wait()
        for way in (0, 1):

            @pl.when(exists(1 - way, 1))
            def _():
                hop(item, way, 0).wait_send()

            for dist in range(1, span):

                @pl.when(exists(way, dist))
                def _():
                    @pl.when(exists(1 - way, 1))
                    def _():
                        hop(item, way, dist).wait_send()

                    across(item, way, dist, side).wait_send()
                    to_core(item, way, dist, me).wait_send()
                    to_core(item, way, dist, partner_core).wait_recv()


def gather_rows(arrays, collective_id):
    seq_size = lax.axis_size("seq")
    fits = lax.axis_size("cfg") == 2 and seq_size <= 8 and seq_size % 2 == 0
    for array in arrays:
        fits = fits and array.shape[1] % 16 == 0 and array.shape[2] % 256 == 0
    if not fits:
        return [lax.all_gather(array, "seq", axis=1, tiled=True) for array in arrays]
    count, span = len(arrays), seq_size // 2
    dma = pltpu.SemaphoreType.DMA
    whole = [(a.shape[0], a.shape[1] * seq_size, a.shape[2]) for a in arrays]
    moved = sum(2 * a.size * seq_size for a in arrays)
    return pl.pallas_call(
        lambda *refs: gather_kernel(count, seq_size, *refs),
        out_shape=[jax.ShapeDtypeStruct(s, jnp.bfloat16) for s in whole],
        in_specs=[pl.BlockSpec(memory_space=pl.ANY)] * count,
        out_specs=[pl.BlockSpec(memory_space=pl.ANY)] * count,
        scratch_shapes=[dma((count, 2, span))] * 6 + [dma((count,))] * 3,
        compiler_params=pltpu.CompilerParams(
            collective_id=collective_id, has_side_effects=True
        ),
        cost_estimate=pl.CostEstimate(flops=0, bytes_accessed=2 * moved, transcendentals=0),
        name="gather_rows",
    )(*arrays)


def body(
    latent,
    img_hidden,
    txt_hidden,
    segments,
    timesteps,
    modulation,
    qk_gain,
    qkv_weight,
    text_weight,
    out_weight,
    expand_weight,
    contract_weight,
    final_weight,
):
    tokens_here = img_hidden.shape[1]
    requests = img_hidden.shape[2]
    feat_width = img_hidden.shape[3]
    head_size = qk_gain.shape[1]
    local_cols = qkv_weight.shape[2]
    heads_here = local_cols // head_size
    text_here = txt_hidden.shape[1]
    modulate = modulation[0]
    hidden = img_hidden[0].astype(jnp.float32)
    image_normed = (layer_norm(hidden) * (1.0 + modulate[:, 1]) + modulate[:, 0]).astype(
        jnp.bfloat16
    )
    row_count = tokens_here * requests
    token_rows = image_normed.reshape(row_count, feat_width)
    segment_row = segments[0]
    one_hot = (segment_row[:, None] == jnp.arange(requests, dtype=jnp.int32)[None, :]).astype(
        jnp.float32
    )
    text_mod = jnp.einsum("tr,rkd->tkd", one_hot, modulate[:, 3:5], precision=lax.Precision.HIGHEST)
    text_normed = (
        layer_norm(txt_hidden[0].astype(jnp.float32)) * (1.0 + text_mod[:, 1]) + text_mod[:, 0]
    ).astype(jnp.bfloat16)
    owner_piece = lax.all_gather(
        segments[0].astype(jnp.float32).astype(jnp.bfloat16), "seq", axis=0, tiled=True
    )
    qkv_full, text_full = gather_rows([qkv_weight, text_weight], 0)
    image_term = jnp.einsum(
        "rd,kdc->rkc", token_rows, qkv_full, preferred_element_type=jnp.float32
    )
    text_term = jnp.einsum(
        "rd,kdc->rkc", text_normed, text_full, preferred_element_type=jnp.float32
    )
    queries = head_norm(
        image_term[:, 0].reshape(tokens_here, requests, heads_here, head_size), qk_gain[0]
    ).astype(jnp.bfloat16)
    keys_img = head_norm(
        image_term[:, 1].reshape(tokens_here, requests, heads_here, head_size), qk_gain[1]
    ).astype(jnp.bfloat16)
    values_img = image_term[:, 2].reshape(tokens_here, requests, local_cols).astype(jnp.bfloat16)
    keys_txt = head_norm(
        text_term[:, 0].reshape(text_here, heads_here, head_size), qk_gain[1]
    ).astype(jnp.bfloat16)
    values_txt = text_term[:, 1].astype(jnp.bfloat16)
    image_pair = jnp.stack(
        [keys_img.reshape(tokens_here, requests, local_cols), values_img], axis=2
    )
    text_pair = jnp.stack([keys_txt.reshape(text_here, local_cols), values_txt], axis=1)
    scale_factor = head_size ** (-0.5)
    request_ids = jnp.arange(requests, dtype=jnp.float32)
    running_max = jnp.full((requests, heads_here, tokens_here), masked_score, jnp.float32)
    image_piece = lax.all_gather(image_pair, "seq", axis=0, tiled=True)
    text_piece = lax.all_gather(text_pair, "seq", axis=0, tiled=True)
    late_weights, _ = lax.optimization_barrier(
        ((out_weight, contract_weight, expand_weight), image_pair)
    )
    late_full = gather_rows(
        [late_weights[0].T[None], late_weights[1].T[None], late_weights[2][None]], 1
    )
    (out_full, contract_full, expand_full), queries = lax.optimization_barrier(
        (tuple(late_full), queries)
    )
    piece_keys = image_piece[:, :, 0].reshape(-1, requests, heads_here, head_size)
    piece_values = image_piece[:, :, 1].reshape(-1, requests, heads_here, head_size)
    text_keys = text_piece[:, 0].reshape(-1, heads_here, head_size)
    text_values = text_piece[:, 1].reshape(-1, heads_here, head_size)
    image_scores = (
        jnp.einsum("qrhd,krhd->rhqk", queries, piece_keys, preferred_element_type=jnp.float32)
        * scale_factor
    )
    text_scores = (
        jnp.einsum("qrhd,khd->rhqk", queries, text_keys, preferred_element_type=jnp.float32)
        * scale_factor
    )
    allowed = owner_piece.astype(jnp.float32)[None, :] == request_ids[:, None]
    text_scores = jnp.where(allowed[:, None, None, :], text_scores, masked_score)
    block_max = jnp.maximum(jnp.max(image_scores, axis=-1), jnp.max(text_scores, axis=-1))
    new_max = jnp.maximum(running_max, block_max)
    image_weights = jnp.exp(image_scores - new_max[..., None])
    text_weights = jnp.exp(text_scores - new_max[..., None])
    new_sum = jnp.sum(image_weights, axis=-1) + jnp.sum(text_weights, axis=-1)
    new_acc = jnp.einsum(
        "rhqk,krhd->rhqd",
        image_weights.astype(jnp.bfloat16),
        piece_values,
        preferred_element_type=jnp.float32,
    )
    new_acc = new_acc + jnp.einsum(
        "rhqk,khd->rhqd",
        text_weights.astype(jnp.bfloat16),
        text_values,
        preferred_element_type=jnp.float32,
    )
    attended = new_acc / new_sum[..., None]
    attended = (
        jnp.transpose(attended, (2, 0, 1, 3)).reshape(row_count, local_cols).astype(jnp.bfloat16)
    )
    share_rows = row_count // lax.axis_size("wgt")
    piece_rows = attended
    mixed = lax.psum_scatter(
        rows_by_rows(piece_rows, out_full[0]).astype(jnp.bfloat16),
        "wgt",
        scatter_dimension=0,
        tiled=True,
    ).astype(jnp.float32)
    tokens_out = share_rows // requests
    row_place = lax.axis_index("wgt") * share_rows
    base_rows = lax.dynamic_slice_in_dim(
        hidden.reshape(row_count, feat_width), row_place, share_rows, 0
    )
    residual = base_rows.reshape(tokens_out, requests, feat_width) + modulate[:, 2] * mixed.reshape(
        tokens_out, requests, feat_width
    )
    branch_in = (layer_norm(residual) * (1.0 + modulate[:, 6]) + modulate[:, 5]).astype(
        jnp.bfloat16
    )
    own_rows = branch_in.reshape(share_rows, feat_width)
    if lax.axis_size("wgt") == 2:
        other_rows = from_partner(own_rows, "wgt", 0)
        is_low = lax.axis_index("wgt") == 0
        branch_rows = jnp.concatenate(
            [
                jnp.where(is_low, own_rows, other_rows),
                jnp.where(is_low, other_rows, own_rows),
            ],
            axis=0,
        )
    else:
        branch_rows = lax.all_gather(own_rows, "wgt", axis=0, tiled=True)
    expanded = jnp.dot(
        branch_rows,
        expand_full[0],
        preferred_element_type=jnp.float32,
    )
    expanded = jax.nn.gelu(expanded, approximate=True).astype(jnp.bfloat16)
    piece_rows = expanded
    branch = lax.psum_scatter(
        rows_by_rows(piece_rows, contract_full[0]).astype(jnp.bfloat16),
        "wgt",
        scatter_dimension=0,
        tiled=True,
    ).astype(jnp.float32)
    second = residual + modulate[:, 7] * branch.reshape(tokens_out, requests, feat_width)
    final_in = (layer_norm(second) * (1.0 + modulate[:, 9]) + modulate[:, 8]).astype(jnp.bfloat16)
    own_velocity = jnp.dot(
        final_in.reshape(share_rows, feat_width), final_weight, preferred_element_type=jnp.float32
    ).reshape(tokens_out, requests, -1)
    guide_side = lax.axis_index("cfg")
    guided_count = latent.shape[1]
    kept_rows = lax.dynamic_slice_in_dim(own_velocity, guide_side * guided_count, guided_count, 1)
    sent_rows = lax.dynamic_slice_in_dim(
        own_velocity, (1 - guide_side) * guided_count, guided_count, 1
    )
    partner_velocity = from_partner(sent_rows, "cfg", 0)
    is_first = guide_side == 0
    conditional = jnp.where(is_first, kept_rows, partner_velocity)
    unconditional = jnp.where(is_first, partner_velocity, kept_rows)
    velocity = unconditional + guidance_scale * (conditional - unconditional)
    step_size = sigma_of(timesteps + 1) - sigma_of(timesteps)
    step_here = lax.dynamic_slice_in_dim(step_size, guide_side * guided_count, guided_count, 0)
    next_latent = latent + step_here[None, :, None] * velocity
    return (velocity, next_latent)


def solution(mesh):
    return jax.shard_map(
        body,
        mesh=mesh,
        in_specs=(
            P(("seq", "wgt"), "cfg", None),
            P("cfg", "seq", None, None),
            P("cfg", "seq", None),
            P("cfg", "seq"),
            P(),
            P("cfg", None, None, None),
            P(),
            P(None, "seq", "wgt"),
            P(None, "seq", "wgt"),
            P("wgt", "seq"),
            P("seq", "wgt"),
            P("wgt", "seq"),
            P(),
        ),
        out_specs=(P(("seq", "wgt"), "cfg", None), P(("seq", "wgt"), "cfg", None)),
        check_vma=False,
    )
```
